32 devices in a mesh: groups: 1, node: 4 (over y, x), ep: 8 (over z, core).
Axes of the slice: x: 2, y: 2, z: 4, core: 2. Of those that a mesh axis runs over, the one named last changes fastest.
Arguments:
- tokens: bfloat16 [2048, 4096], P(('groups', 'node', 'ep')), may hold values from -6 to 6
- expert_ids: int32 [2048, 8], P(('groups', 'node', 'ep')), may hold values from 0 to 15, all different within a row; in each aligned block of 64 rows (0 to 63, 64 to 127, ...) at most 48 rows name the same one
- gate_values: float32 [2048, 8], P(('groups', 'node', 'ep')), may hold values from 0.1 to 1
- gate_weight: bfloat16 [32, 2048, 768], P(('node', 'ep')), may hold values from -0.09375 to 0.09375
- up_weight: bfloat16 [32, 2048, 768], P(('node', 'ep')), may hold values from -0.09375 to 0.09375
- down_weight: bfloat16 [32, 768, 2048], P(('node', 'ep')), may hold values from -0.21875 to 0.21875
Outputs:
- mixed: bfloat16 [2048, 4096], P(('groups', 'node', 'ep'))
The draws below stay inside these ranges and needn't reach their ends.
Inputs may be any that keep to these rules, and one draw needn't show every extreme that they name: `expert_ids`: each row names 8 different experts. In the 64 rows of one device no expert is named more than 48 times, and in every draw some device names some expert exactly 48 times.
All inputs are finite; a program needn't handle non-finite values.
Results may differ from the reference program's by a relative error of at most 0.017.
Values may be sent and summed in bfloat16 or wider, within the bound.
A program may use at most 128 MiB of HBM per device.

```python
import math
import jax
import jax.numpy as jnp
import numpy as np
from jax import lax

D = 4096
FF = 768
QB = 128
TOP = 8
TOK_DEV = 64
EXPERTS = 16
CAP = 48
TOKENS = 2048
N_NODE = 4
N_EP = 8


def steps_of(rng, extent, split, low, high):
    factor_of = 1.0
    for axis_at, shards_of in split:
        heights = jax.random.uniform(jax.random.fold_in(jax.random.fold_in(rng, 6), axis_at), (shards_of,), jnp.float32, low / len(split), high / len(split))
        factor_of = factor_of * jnp.repeat(jnp.exp(heights), extent[axis_at] // shards_of).reshape((-1,) + (1,) * (len(extent) - 1 - axis_at))
    return factor_of


def shared_out(rng, own, number, rows, count, top, reach, skew):
    order = jax.random.permutation(rng, count)
    heavy_load, common = portions_of(count, rows * top, reach, skew, True), portions_of(count, rows * top, reach, skew, False)
    places = jnp.arange(count)

    def named(tallies, turn):
        used = int((tallies > 0).sum())
        fixed = max(1, used // 4)
        moved = fixed + (places - fixed + turn * (used - fixed)) % max(1, count - fixed)
        return jnp.zeros((count,), jnp.int32).at[order[jnp.where(places < fixed, places, moved)]].set(jnp.asarray(tallies, jnp.int32))

    tallies = jnp.where(number % 4 == 0, named(heavy_load, number // 4), named(common, number - number // 4 - 1))
    mixed = jax.random.permutation(jax.random.fold_in(own, 3), count)
    donor, receiver = mixed[0:count // 2 * 2:2], mixed[1:count // 2 * 2:2]
    slack = jnp.minimum(tallies[donor] - 1, reach - tallies[receiver]) // 2
    slack = jnp.where((donor == order[0]) | (receiver == order[0]) | (tallies[receiver] == 0), 0, jnp.maximum(slack, 0))
    moved = jax.random.randint(jax.random.fold_in(own, 4), (count // 2,), 0, 1 << 20) % (slack + 1)
    tallies = tallies.at[donor].add(-moved).at[receiver].add(moved)
    items = jnp.searchsorted(jnp.cumsum(tallies), jnp.arange(rows * top), side="right").astype(jnp.int32)
    listing = items.reshape(top, rows).T
    listing = listing[jax.random.permutation(jax.random.fold_in(own, 1), rows)]
    turn = jax.random.randint(jax.random.fold_in(own, 2), (rows, 1), 0, top)
    return jnp.take_along_axis(listing, (jnp.arange(top)[None, :] + turn) % top, axis=1)


def portions_of(amount, total, bound, slope, full):
    loads = [(1 << 20) // math.isqrt(grade ** slope) + 1 for grade in range(1, amount + 1)]
    largest = bound if full else min(bound, max(-(-total // amount), total * loads[0] // sum(loads)))
    least = 1 if total - largest >= amount - 1 else 0
    given, surplus = [largest] + [least] * (amount - 1), total - largest - least * (amount - 1)
    while surplus > 0:
        movable = [i for i in range(1, amount) if given[i] < largest] or [i for i in range(1, amount) if given[i] < bound]
        mass, budget = sum([loads[i] for i in movable]), surplus
        for i in movable:
            more = min(bound - given[i], max(1, budget * loads[i] // mass), surplus)
            given[i] = given[i] + more
            surplus = surplus - more
    return np.array(given)


def bell_draw(own_key, dims, scale, most, cuts=(), kind=jnp.bfloat16):
    entries = scale * jax.random.normal(own_key, dims, jnp.float32)
    if cuts:
        entries = entries * steps_of(own_key, dims, cuts, -0.22, 0.18)
    return jnp.clip(entries, -most, most).astype(kind)


def setup_inputs(seed: int = 0, part: int = 0) -> dict:
    keys = jax.random.split(jax.random.key(seed), 7)
    part_splits = jax.random.split(jax.random.fold_in(keys[6], part), 7)
    tokens = bell_draw(part_splits[0], (TOKENS, D), 1.0, 6.0, ((0, 32),))
    expert_ids_keys = jax.random.split(jax.random.fold_in(part_splits[1], 1), TOKENS // TOK_DEV)
    expert_ids_turns = jax.random.permutation(jax.random.fold_in(part_splits[1], 3), TOKENS // TOK_DEV)
    expert_ids = jax.vmap(lambda own, number: shared_out(jax.random.fold_in(part_splits[1], 2), own, number, TOK_DEV, EXPERTS, TOP, CAP, 2))(expert_ids_keys, expert_ids_turns).reshape((TOKENS, TOP))
    gate_values = jnp.clip(0.1 + 0.9 * jax.random.uniform(part_splits[2], (TOKENS, TOP), jnp.float32) ** steps_of(part_splits[2], (TOKENS, TOP), ((0, 32),), -0.2, 0.2), 0.1, 1.0)
    gate_weight = bell_draw(keys[3], (N_NODE * N_EP, D // 2, FF), D ** -0.5, 0.09375, ((0, 32),))
    up_weight = bell_draw(keys[4], (N_NODE * N_EP, D // 2, FF), D ** -0.5, 0.09375, ((0, 32),))
    down_weight = bell_draw(keys[5], (N_NODE * N_EP, FF, D // 2), FF ** -0.5, 0.21875, ((0, 32),))
    return {"tokens": tokens, "expert_ids": expert_ids, "gate_values": gate_values, "gate_weight": gate_weight, "up_weight": up_weight, "down_weight": down_weight}


def quantize(tokens):
    row_count, model_width = tokens.shape
    scaled = tokens.astype(jnp.float32).reshape(row_count, model_width // QB, QB)
    largest = jnp.max(jnp.abs(scaled), axis=2)
    block_scales = ((largest + 1e-6) / 448.0).astype(jnp.bfloat16)
    quantized = (scaled / block_scales.astype(jnp.float32)[:, :, None]).astype(jnp.bfloat16)
    return quantized.reshape(row_count, model_width), block_scales


def slot_positions(flat_ids, expert_count):
    matches = (flat_ids[..., None] == jnp.arange(expert_count, dtype=jnp.int32)).astype(jnp.int32)
    running = jnp.cumsum(matches, axis=-2)
    return jnp.sum(matches * running, axis=-1) - 1


def reference(tokens, expert_ids, gate_values, gate_weight, up_weight, down_weight):
    quantized, block_scales = quantize(tokens)
    restored = (quantized.astype(jnp.float32).reshape(TOKENS, D // QB, QB)
                * block_scales.astype(jnp.float32)[:, :, None]).reshape(TOKENS, D).astype(jnp.bfloat16)
    restored = jnp.concatenate([restored, jnp.zeros((1, D), jnp.bfloat16)], axis=0)
    device_count = N_NODE * N_EP
    flat_ids = expert_ids.reshape(device_count, TOK_DEV * TOP)
    positions_in = slot_positions(flat_ids, EXPERTS)
    token_index = (jnp.arange(device_count * TOK_DEV * TOP, dtype=jnp.int32) // TOP).reshape(device_count, TOK_DEV * TOP)
    source = jnp.arange(device_count, dtype=jnp.int32)[:, None]
    position = ((flat_ids * device_count + source) * CAP + positions_in).reshape(-1)
    slot_table = jnp.full((EXPERTS * device_count * CAP,), TOKENS, jnp.int32).at[position].set(token_index.reshape(-1))
    route_weights = jnp.zeros((EXPERTS * device_count * CAP,), jnp.float32).at[position].set(gate_values.reshape(-1))
    slot_table = slot_table.reshape(EXPERTS, device_count * CAP)
    route_weights = route_weights.reshape(EXPERTS, device_count * CAP)
    gate_full = gate_weight.reshape(EXPERTS, D, FF)
    up_full = up_weight.reshape(EXPERTS, D, FF)
    down_pairs = down_weight.reshape(EXPERTS, 2, FF, D // 2)

    def one_expert(totals, inputs):
        rows_index, row_weights, gate_matrix, up_matrix, down_matrix = inputs
        chosen = restored[rows_index]
        gate_sum = jnp.dot(chosen, gate_matrix, preferred_element_type=jnp.float32)
        up_sum = jnp.dot(chosen, up_matrix, preferred_element_type=jnp.float32)
        hidden = (jax.nn.silu(gate_sum) * up_sum).astype(jnp.bfloat16)
        down_full = jnp.concatenate([down_matrix[0], down_matrix[1]], axis=1)
        expert_out = jnp.dot(hidden, down_full, preferred_element_type=jnp.float32).astype(jnp.bfloat16)
        return totals.at[rows_index].add(row_weights[:, None] * expert_out.astype(jnp.float32)), None

    totals, _ = lax.scan(one_expert, jnp.zeros((TOKENS + 1, D), jnp.float32),
                         (slot_table, route_weights, gate_full, up_full, down_pairs))
    return totals[:TOKENS].astype(jnp.bfloat16)
```

```python
import functools

import jax
import jax.numpy as jnp
from jax import lax
from jax.experimental import pallas as pl
from jax.experimental.pallas import tpu as pltpu
from jax.sharding import PartitionSpec as P

LANES = 128


def partner(array, axis, stride):
    return lax.ppermute(array, axis, [(i, i ^ 1 << stride) for i in range(lax.axis_size(axis))])


def quantize(tokens):
    row_count, model_width = tokens.shape
    scaled = tokens.astype(jnp.float32).reshape(row_count, model_width // 128, 128)
    largest = jnp.max(jnp.abs(scaled), axis=2)
    block_scales = ((largest + 1e-06) / 448.0).astype(jnp.bfloat16)
    quantized = (scaled / block_scales.astype(jnp.float32)[:, :, None]).astype(jnp.bfloat16)
    return (quantized.reshape(row_count, model_width), block_scales)


def slot_positions(flat_ids, expert_count):
    matches = (flat_ids[..., None] == jnp.arange(expert_count, dtype=jnp.int32)).astype(jnp.int32)
    running = jnp.cumsum(matches, axis=-2)
    return jnp.sum(matches * running, axis=-1) - 1


def restore(pieces):
    quantized, block_scales = pieces
    leading = quantized.shape[:2]
    row_width = quantized.shape[2]
    block_count = block_scales.shape[2]
    scaled = quantized.astype(jnp.float32).reshape(
        leading + (block_count, row_width // block_count)
    )
    scaled = scaled * block_scales.astype(jnp.float32)[..., None]
    return (scaled.reshape(-1, row_width).astype(jnp.bfloat16), leading)


def expert_rows(pieces, gate_half, up_half, down_half):
    restored, leading = restore(pieces)
    gate_part = jnp.dot(restored, gate_half, preferred_element_type=jnp.float32)
    up_part = jnp.dot(restored, up_half, preferred_element_type=jnp.float32)
    gate_other, up_other = partner((gate_part, up_part), "ep", 0)
    gate_sum = gate_part + gate_other
    up_sum = up_part + up_other
    hidden = (jax.nn.silu(gate_sum) * up_sum).astype(jnp.bfloat16)
    result = jnp.dot(hidden, down_half, preferred_element_type=jnp.float32).astype(jnp.bfloat16)
    return result.reshape(leading + (down_half.shape[1],))


def on_device(tokens, expert_ids, gate_values, gate_weight, up_weight, down_weight):
    row_count, model_width = tokens.shape
    route_count = expert_ids.shape[1]
    half_width = model_width // 2
    node_count = lax.axis_size("node")
    owner_count = lax.axis_size("ep")
    device_count = node_count * owner_count
    expert_count = device_count // 2
    capacity = min(row_count, 3 * row_count * route_count // (2 * expert_count))
    quantized, block_scales = quantize(tokens)
    block_total = block_scales.shape[1]
    half_blocks = block_total // 2
    flat_ids = expert_ids.reshape(-1)
    positions_in = slot_positions(flat_ids, expert_count)
    route_total = row_count * route_count
    token_index = jnp.arange(route_total, dtype=jnp.int32) // route_count
    slot_table = jnp.full((expert_count * capacity,), row_count, jnp.int32)
    slot_table = slot_table.at[flat_ids * capacity + positions_in].set(token_index)
    half_index = jnp.arange(2, dtype=jnp.int32)
    quant_rows = jnp.concatenate(
        [
            quantized.reshape(row_count, 2, half_width).swapaxes(0, 1),
            jnp.zeros((2, 1, half_width), jnp.bfloat16),
        ],
        axis=1,
    ).reshape(2 * (row_count + 1), half_width)
    scale_rows = jnp.concatenate(
        [
            block_scales.reshape(row_count, 2, half_blocks).swapaxes(0, 1),
            jnp.zeros((2, 1, half_blocks), jnp.bfloat16),
        ],
        axis=1,
    ).reshape(2 * (row_count + 1), half_blocks)
    picked = (
        half_index[None, :, None] * (row_count + 1) + slot_table.reshape(expert_count, 1, capacity)
    ).reshape(device_count, capacity)
    sent_quant = quant_rows[picked]
    sent_scales = scale_rows[picked]
    outputs = expert_rows(
        (
            lax.all_to_all(sent_quant, ("node", "ep"), split_axis=0, concat_axis=0, tiled=True),
            lax.all_to_all(sent_scales, ("node", "ep"), split_axis=0, concat_axis=0, tiled=True),
        ),
        gate_weight[0],
        up_weight[0],
        down_weight[0],
    )
    returned = lax.all_to_all(outputs, ("node", "ep"), split_axis=0, concat_axis=0, tiled=True)
    paired = returned.reshape(expert_count, 2, capacity, half_width)
    gathered = paired[flat_ids, :, positions_in].reshape(route_total, model_width)
    weighted = gathered.astype(jnp.float32) * gate_values.reshape(-1)[:, None]
    mixed = jnp.sum(weighted.reshape(row_count, route_count, model_width), axis=1)
    return mixed.astype(jnp.bfloat16)


def dense_kernel(
    line_count,
    tokens_ref,
    ids_ref,
    gates_ref,
    gate_hbm,
    up_hbm,
    down_hbm,
    out_ref,
    x_buf,
    part_buf,
    diag_buf,
    line_buf,
    final_buf,
    gate_w,
    up_w,
    down_w,
    hidden,
    w_local,
    w_send,
    w_recv,
    z_send,
    z_recv,
    n_send,
    n_recv,
    d_send,
    d_recv,
    e_send,
    e_recv,
    f_send,
    f_recv,
    g_send,
    g_recv,
    h_send,
    h_recv,
):
    node, ep = lax.axis_index("node"), lax.axis_index("ep")
    core, z = lax.rem(ep, 2), ep // 2
    expert = node * line_count + z
    row_count, width = tokens_ref.shape
    half_rows = row_count // 2
    half_width = width // 2
    route_count = ids_ref.shape[1]
    expert_count = 4 * line_count
    hidden_width = gate_w.shape[2]
    batch = 2 * line_count * half_rows

    x_peer = {"node": node + 1 - 2 * lax.rem(node, 2), "ep": ep}
    y_peer = {"node": lax.rem(node + 2, 4), "ep": ep}
    core_peer = {"node": node, "ep": ep + 1 - 2 * core}
    sides = (x_peer, y_peer)

    def z_peer(j):
        return {"node": node, "ep": 2 * lax.rem(z + j, line_count) + core}

    def slot(j):
        return lax.rem(z + line_count - j, line_count)

    def remote(src, dst, send, recv, device):
        copy = pltpu.make_async_remote_copy(
            src_ref=src,
            dst_ref=dst,
            send_sem=send,
            recv_sem=recv,
            device_id=device,
            device_id_type=pl.DeviceIdType.MESH,
        )
        copy.start()
        started.append(copy)
        return copy

    started = []
    weights = ((gate_hbm, gate_w), (up_hbm, up_w), (down_hbm, down_w))
    barrier = pltpu.get_barrier_semaphore()
    peers = [x_peer, y_peer, core_peer] + [z_peer(j) for j in range(1, line_count)]
    for peer in peers:
        pl.semaphore_signal(barrier, inc=1, device_id=peer, device_id_type=pl.DeviceIdType.MESH)
    local = []
    for i, (hbm, held) in enumerate(weights):
        copy = pltpu.make_async_copy(hbm.at[0], held.at[core], w_local.at[i])
        copy.start()
        local.append(copy)

    def restore_block(b, carry):
        columns = pl.ds(pl.multiple_of(b * LANES, LANES), LANES)
        block = tokens_ref[:, columns].astype(jnp.float32)
        largest = jnp.max(jnp.abs(block), axis=1, keepdims=True)
        scale = ((largest + 1e-06) / 448.0).astype(jnp.bfloat16).astype(jnp.float32)
        quantized = (block / scale).astype(jnp.bfloat16).astype(jnp.float32)
        restored = (quantized * scale).astype(jnp.bfloat16)
        x_buf[0, :, z, :, columns] = restored.reshape(2, half_rows, LANES)
        return carry

    lax.fori_loop(0, width // LANES, restore_block, 0, unroll=4)
    lane = lax.broadcasted_iota(jnp.int32, (row_count, LANES), 1)
    lane_expert = lax.rem(lane, expert_count)
    table = jnp.zeros((row_count, LANES), jnp.float32)
    for k in range(route_count):
        table = table + jnp.where(ids_ref[:, k : k + 1] == lane_expert, gates_ref[:, k : k + 1], 0.0)
    high = table.astype(jnp.bfloat16).astype(jnp.float32)
    middle = (table - high).astype(jnp.bfloat16).astype(jnp.float32)
    low = table - high - middle
    pieces = jnp.where(
        lane < expert_count,
        high,
        jnp.where(lane < 2 * expert_count, middle, jnp.where(lane < 3 * expert_count, low, 0.0)),
    )
    x_buf[0, :, z, :, width : width + LANES] = pieces.astype(jnp.bfloat16).reshape(
        2, half_rows, LANES
    )
    pl.semaphore_wait(barrier, len(peers))

    along = [
        remote(x_buf.at[0, :, z], x_buf.at[0, :, z], z_send.at[j - 1], z_recv.at[j - 1], z_peer(j))
        for j in range(1, line_count)
    ]
    across = []
    for j in range(line_count):
        if j > 0:
            along[j - 1].wait_recv()
        for s in range(2):
            across.append(
                remote(
                    x_buf.at[0, :, slot(j)],
                    x_buf.at[s + 1, :, slot(j)],
                    n_send.at[s, j],
                    n_recv.at[s, j],
                    sides[s],
                )
            )
        if j == 0:
            moved = [
                remote(hbm.at[0], held.at[core], w_send.at[i], w_recv.at[i], core_peer)
                for i, (hbm, held) in enumerate(weights)
            ]
    for i in range(3):
        local[i].wait()
        moved[i].wait_recv()

    def run_expert(group):
        def hidden_tile(n, carry):
            columns = pl.ds(pl.multiple_of(n * 256, 256), 256)
            sums = []
            for held in (gate_w, up_w):
                total = None
                for h in range(2):
                    rows = x_buf[group, :, :, :, h * half_width : (h + 1) * half_width]
                    term = jnp.dot(
                        rows.reshape(batch, half_width),
                        held[h, :, columns],
                        preferred_element_type=jnp.float32,
                    )
                    total = term if total is None else total + term
                sums.append(total)
            gate_sum, up_sum = sums
            act = gate_sum / (1.0 + jnp.exp(-gate_sum))
            hidden[:, columns] = (act * up_sum).astype(jnp.bfloat16)
            return carry

        lax.fori_loop(0, hidden_width // 256, hidden_tile, 0)
        spread = x_buf[group, :, :, :, width : width + LANES].reshape(batch, LANES)
        lanes = lax.broadcasted_iota(jnp.int32, (batch, LANES), 1)
        weight = jnp.sum(
            jnp.where(lax.rem(lanes, expert_count) == expert, spread.astype(jnp.float32), 0.0),
            axis=1,
            keepdims=True,
        )

        for h in range(2):

            def out_tile(n, carry):
                columns = pl.ds(pl.multiple_of(n * 256, 256), 256)
                result = jnp.dot(
                    hidden[...], down_w[h, :, columns], preferred_element_type=jnp.float32
                )
                result = result.astype(jnp.bfloat16).astype(jnp.float32) * weight
                target = pl.ds(pl.multiple_of(h * half_width + n * 256, 256), 256)
                part_buf[group, :, :, :, target] = result.astype(jnp.bfloat16).reshape(
                    2, line_count, half_rows, 256
                )
                return carry

            lax.fori_loop(0, half_width // 256, out_tile, 0)

    def add_into(target, terms):
        def columns_of(n, carry):
            columns = pl.ds(pl.multiple_of(n * 512, 512), 512)
            index = (Ellipsis, columns)
            total = terms[0][index].astype(jnp.float32)
            for term in terms[1:]:
                total = total + term[index].astype(jnp.float32)
            target[index] = total.astype(jnp.bfloat16)
            return carry

        lax.fori_loop(0, width // 512, columns_of, 0)

    run_expert(0)
    corner = []
    for j in range(line_count):
        for s in range(2):
            across[2 * j + s].wait_recv()
            corner.append(
                remote(
                    x_buf.at[s + 1, s, slot(j)],
                    x_buf.at[3, s, slot(j)],
                    d_send.at[s, j],
                    d_recv.at[s, j],
                    sides[1 - s],
                )
            )
    early = []
    for s in range(2):
        run_expert(s + 1)
        early.append(
            remote(
                part_buf.at[s + 1, s], line_buf.at[s, s], e_send.at[s], e_recv.at[s], sides[s]
            )
        )
    for copy in corner:
        copy.wait_recv()
    run_expert(3)
    turned, late, home = {}, {}, []
    order = list(range(1, line_count)) + [0]
    for j in order:
        for s in range(2):
            turned[j, s] = remote(
                part_buf.at[3, s, slot(j)],
                diag_buf.at[s, slot(j)],
                f_send.at[s, j],
                f_recv.at[s, j],
                sides[s],
            )
    for s in range(2):
        early[s].wait_recv()
    for j in order:
        for s in range(2):
            turned[j, s].wait_recv()
            add_into(
                part_buf.at[2 - s, s, slot(j)],
                [part_buf.at[2 - s, s, slot(j)], diag_buf.at[s, slot(j)]],
            )
            late[j, s] = remote(
                part_buf.at[2 - s, s, slot(j)],
                line_buf.at[1 - s, s, slot(j)],
                g_send.at[s, j],
                g_recv.at[s, j],
                sides[1 - s],
            )
    for j in order:
        for s in range(2):
            late[j, s].wait_recv()
        if j > 0:
            add_into(
                part_buf.at[0, :, slot(j)],
                [part_buf.at[0, :, slot(j)]] + [line_buf.at[s, :, slot(j)] for s in range(2)],
            )
            home.append(
                remote(
                    part_buf.at[0, :, slot(j)],
                    final_buf.at[j - 1],
                    h_send.at[j - 1],
                    h_recv.at[j - 1],
                    z_peer(line_count - j),
                )
            )
    for copy in home:
        copy.wait_recv()

    def finish(n, carry):
        columns = pl.ds(pl.multiple_of(n * 256, 256), 256)
        total = part_buf[0, :, z, :, columns].astype(jnp.float32)
        for s in range(2):
            total = total + line_buf[s, :, z, :, columns].astype(jnp.float32)
        for j in range(1, line_count):
            total = total + final_buf[j - 1, :, :, columns].astype(jnp.float32)
        out_ref[:, columns] = total.astype(jnp.bfloat16).reshape(row_count, 256)
        return carry

    lax.fori_loop(0, width // 256, finish, 0)
    for copy in started:
        copy.wait_send()


def dense_on_device(tokens, expert_ids, gate_values, gate_weight, up_weight, down_weight):
    row_count, model_width = tokens.shape
    hidden_width = gate_weight.shape[2]
    lines = lax.axis_size("ep") // 2
    half_rows = row_count // 2
    half_width = model_width // 2
    vmem = pl.BlockSpec(memory_space=pltpu.VMEM)
    anywhere = pl.BlockSpec(memory_space=pl.ANY)
    dma = pltpu.SemaphoreType.DMA
    return pl.pallas_call(
        functools.partial(dense_kernel, lines),
        out_shape=jax.ShapeDtypeStruct((row_count, model_width), jnp.bfloat16),
        in_specs=[vmem] * 3 + [anywhere] * 3,
        out_specs=vmem,
        scratch_shapes=[
            pltpu.VMEM((4, 2, lines, half_rows, model_width + LANES), jnp.bfloat16),
            pltpu.VMEM((4, 2, lines, half_rows, model_width), jnp.bfloat16),
            pltpu.VMEM((2, lines, half_rows, model_width), jnp.bfloat16),
            pltpu.VMEM((2, 2, lines, half_rows, model_width), jnp.bfloat16),
            pltpu.VMEM((lines - 1, 2, half_rows, model_width), jnp.bfloat16),
            pltpu.VMEM((2, half_width, hidden_width), jnp.bfloat16),
            pltpu.VMEM((2, half_width, hidden_width), jnp.bfloat16),
            pltpu.VMEM((2, hidden_width, half_width), jnp.bfloat16),
            pltpu.VMEM((2 * lines * half_rows, hidden_width), jnp.bfloat16),
            dma((3,)),
            dma((3,)),
            dma((3,)),
            dma((lines - 1,)),
            dma((lines - 1,)),
            dma((2, lines)),
            dma((2, lines)),
            dma((2, lines)),
            dma((2, lines)),
            dma((2,)),
            dma((2,)),
            dma((2, lines)),
            dma((2, lines)),
            dma((2, lines)),
            dma((2, lines)),
            dma((lines - 1,)),
            dma((lines - 1,)),
        ],
        compiler_params=pltpu.CompilerParams(
            collective_id=0, has_side_effects=True, vmem_limit_bytes=60 * 1024 * 1024
        ),
    )(tokens, expert_ids, gate_values, gate_weight, up_weight, down_weight)


def solution(mesh):
    in_specs = (
        P(("groups", "node", "ep"), None),
        P(("groups", "node", "ep"), None),
        P(("groups", "node", "ep"), None),
        P(("node", "ep"), None, None),
        P(("node", "ep"), None, None),
        P(("node", "ep"), None, None),
    )
    out_specs = P(("groups", "node", "ep"), None)
    few = mesh.shape["node"] == 4 and mesh.shape["ep"] <= 8
    return jax.shard_map(
        dense_on_device if few else on_device, mesh=mesh, in_specs=in_specs, out_specs=out_specs, check_vma=False
    )
```
